128 devices in a mesh: morton: 128 (over y, z, x, core).
Axes of the slice: x: 4, y: 4, z: 4, core: 2. Of those that a mesh axis runs over, the one named last changes fastest.
Arguments:
- leaf_mult: bfloat16 [98304, 152], P('morton'), may hold values from -6 to 6
- leaf_list: int32 [98304, 316], P('morton'), may hold values from -6144 to 6144, as said below
- parent_list: int32 [12288, 316], P('morton'), may hold values from -1 to 12287, as said below
- top_list: int32 [1536, 316], P('morton'), may hold values from -1 to 1535, as said below
- m2m_ops: bfloat16 [8, 152, 152], replicated, may hold values from -0.15625 to 0.15625
- m2l_ops: bfloat16 [316, 152, 152], replicated, may hold values from -0.0390625 to 0.0390625
- l2l_ops: bfloat16 [8, 152, 152], replicated, may hold values from -0.5 to 0.5
Outputs:
- leaf_local: float32 [98304, 152], P('morton')
The draws below stay inside these ranges and needn't reach their ends.
Inputs may be any that keep to these rules, and one draw needn't show every extreme that they name: `leaf_list`: 0 marks an empty slot; any other entry is an offset of at most 6144 in size to a leaf box inside the grid, every row has an entry of exactly that size, and both signs occur. `parent_list`: -1 marks an empty slot; any other entry is a parent-level box at most 768 positions from the row's box, and every row has an entry at exactly that distance. `top_list`: -1 marks an empty slot; other entries are any top-level box.
All inputs are finite; a program needn't handle non-finite values.
Results may differ from the reference program's by a relative error of at most 0.0035.
Values may be sent and summed in bfloat16 or wider, within the bound.
No kernel may reach another device: no remote copies, remote signals or barrier semaphores. Data moves between devices by JAX's collectives and lax.ppermute only.
A program may use at most 256 MiB of HBM per device.

```python
import math
import jax
import jax.numpy as jnp
from jax import lax

P_SIZE = 152
NV = 316
BOX_DEV = 768
RD = 8
NB = 98304
NPB = 12288
NT = 1536


def near_rows(key, count, reach):
    keys = jax.random.split(key, 5)
    box = jnp.arange(count, dtype=jnp.int32)
    offset = jax.random.randint(keys[0], (count, NV), -reach, reach + 1, dtype=jnp.int32)
    source = box[:, None] + offset
    share = jax.random.randint(keys[1], (count,), 30, 91, dtype=jnp.int32)
    live = jax.random.randint(keys[2], (count, NV), 0, 100, dtype=jnp.int32) < share[:, None]
    live = live & (source >= 0) & (source < count) & (offset != 0)
    sign = jax.random.randint(keys[3], (count,), 0, 2, dtype=jnp.int32) * 2 - 1
    sign = jnp.where(box == count - 1 - reach, 1, sign)
    edge = box + sign * reach
    edge = jnp.where((edge >= 0) & (edge < count), edge, box - sign * reach)
    slot = jax.random.randint(keys[4], (count,), 0, NV, dtype=jnp.int32)
    picked = jnp.arange(NV, dtype=jnp.int32)[None, :] == slot[:, None]
    source = jnp.where(picked, edge[:, None], source)
    live = live | picked
    return jnp.where(live, source, -1).astype(jnp.int32)


def draw_leaf_list(key, part):
    key = jax.random.fold_in(key, 1)
    source = near_rows(key, NB, RD * BOX_DEV)
    rows = jnp.arange(NB, dtype=jnp.int32)[:, None]
    return jnp.where(source >= 0, source - rows, 0).astype(jnp.int32)


def draw_parent_list(key, part):
    key = jax.random.fold_in(key, 2)
    return near_rows(key, NPB, RD * (BOX_DEV // 8))


def draw_top_list(key, part):
    key = jax.random.fold_in(key, 3)
    keys = jax.random.split(key, 3)
    source = jax.random.randint(keys[0], (NT, NV), 0, NT, dtype=jnp.int32)
    share = jax.random.randint(keys[1], (NT,), 30, 91, dtype=jnp.int32)
    live = jax.random.randint(keys[2], (NT, NV), 0, 100, dtype=jnp.int32) < share[:, None]
    source = source.at[0, 0].set(NT - 1)
    live = live.at[0, 0].set(True)
    live = live.at[NT - 1, NV - 1].set(False)
    return jnp.where(live, source, -1).astype(jnp.int32)


def block_scale(rng, dims, shards, smallest, largest):
    loudness = 1.0
    for position, parts in shards:
        steps = jax.random.uniform(jax.random.fold_in(jax.random.fold_in(rng, 6), position), (parts,), jnp.float32, smallest / len(shards), largest / len(shards))
        loudness = loudness * jnp.repeat(jnp.exp(steps), dims[position] // parts).reshape((-1,) + (1,) * (len(dims) - 1 - position))
    return loudness


def scatter_about(rng, dims, scale, bound, shards=(), kind=jnp.bfloat16):
    gain = block_scale(rng, dims, shards, -0.22, 0.18) if shards else 1.0
    array = jax.random.normal(rng, dims, jnp.float32) * scale * gain
    return jnp.minimum(jnp.maximum(array, -bound), bound).astype(kind)


def setup_inputs(seed: int = 0) -> dict:
    seeds = jax.random.split(jax.random.key(seed), 8)
    return {
        "leaf_mult": scatter_about(seeds[0], (NB, P_SIZE), 1.0, 6.0, ((0, 128),)),
        "leaf_list": draw_leaf_list(jax.random.fold_in(seeds[7], 71), 0),
        "parent_list": draw_parent_list(jax.random.fold_in(seeds[7], 71), 0),
        "top_list": draw_top_list(jax.random.fold_in(seeds[7], 71), 0),
        "m2m_ops": scatter_about(seeds[4], (8, P_SIZE, P_SIZE), (8 * P_SIZE) ** -0.5, 0.15625),
        "m2l_ops": scatter_about(seeds[5], (NV, P_SIZE, P_SIZE), (P_SIZE * NV // 2) ** -0.5, 0.0390625),
        "l2l_ops": scatter_about(seeds[6], (8, P_SIZE, P_SIZE), P_SIZE ** -0.5, 0.5),
    }


def ascend(children, m2m_ops):
    grouped = children.reshape(children.shape[0] // 8, 8, P_SIZE).astype(jnp.float32)
    summed = jnp.einsum("bcq,cqp->bp", grouped, m2m_ops.astype(jnp.float32))
    return summed.astype(jnp.bfloat16)


def descend(coarse, l2l_ops):
    spread = jnp.einsum("tq,cqp->tcp", coarse.astype(jnp.float32), l2l_ops.astype(jnp.float32))
    return spread.reshape(coarse.shape[0] * 8, P_SIZE)


def translate(lists, table, flat_ops):
    count = lists.shape[0]
    block = math.gcd(128, count)

    def one_block(entries):
        live = entries >= 0
        picked = jnp.take(table, jnp.where(live, entries, 0).astype(jnp.int32), axis=0)
        picked = jnp.where(live[:, :, None], picked, jnp.zeros((), table.dtype))
        return jnp.dot(picked.reshape(block, NV * P_SIZE), flat_ops, preferred_element_type=jnp.float32)

    out = lax.map(one_block, lists.reshape(count // block, block, NV))
    return out.reshape(count, P_SIZE)


def reference(leaf_mult, leaf_list, parent_list, top_list, m2m_ops, m2l_ops, l2l_ops):
    flat_ops = m2l_ops.reshape(NV * P_SIZE, P_SIZE)
    rows = jnp.arange(NB, dtype=jnp.int32)[:, None]
    leaf_source = jnp.where(leaf_list != 0, rows + leaf_list, -1).astype(jnp.int32)
    parent_mult = ascend(leaf_mult, m2m_ops)
    top_mult = ascend(parent_mult, m2m_ops)
    top_local = (0.25 * translate(top_list, top_mult, flat_ops)).astype(jnp.bfloat16)
    parent_local = (0.5 * translate(parent_list, parent_mult, flat_ops) + descend(top_local, l2l_ops)).astype(jnp.bfloat16)
    return translate(leaf_source, leaf_mult, flat_ops) + descend(parent_local, l2l_ops)
```

```python
import jax
import jax.numpy as jnp
from jax import lax
from jax.experimental import pallas as pl
from jax.experimental.pallas import tpu as pltpu
from jax.sharding import PartitionSpec as P

RD = 8
PAD = 8


def shifted(block, axis, distance):
    devices = range(lax.axis_size(axis))
    route = [(i - distance, i) for i in devices if i - distance in devices]
    return lax.ppermute(block, axis, route)


def ascend(children, m2m_ops):
    width = children.shape[1]
    grouped = children.reshape(children.shape[0] // 8, 8 * width)
    summed = jnp.dot(grouped, m2m_ops.reshape(8 * width, width), preferred_element_type=jnp.float32)
    return summed.astype(jnp.bfloat16)


def descend(coarse, l2l_ops):
    spread = jnp.einsum("tq,cqp->tcp", coarse, l2l_ops, preferred_element_type=jnp.float32)
    return spread.reshape(coarse.shape[0] * 8, coarse.shape[1])


def far_kernel(slots, near, top, w_ref, out_ref, table, rows_a, rows_b, stage, slots_a, slots_b, sem, stage_sem):
    step = pl.program_id(0)
    steps = pl.num_programs(0)
    count, width = out_ref.shape
    chunk = stage.shape[1]
    top_chunk = top.shape[1]

    def slot_copy(pair, which, buffer):
        return pltpu.make_async_copy(slots.at[pair], buffer, sem.at[which])

    def fill(buffer, base, rows):
        def group(j, carry):
            x = buffer[pl.ds(pl.multiple_of(16 * j, 16), 16), :].astype(jnp.float32)
            tail = jnp.concatenate([x[:, 128:], jnp.zeros((16, 256 - width), jnp.float32)], axis=1)
            start = 2 * (base + 16 * j)
            table[pl.ds(start, 16, stride=2), :] = x[:, :128]
            table[pl.ds(start + 1, 16, stride=2), :] = tail
            return carry

        lax.fori_loop(0, rows // 16, group, 0, unroll=2)

    @pl.when(step == 0)
    def _():
        slot_copy(0, 0, slots_a).start()
        slot_copy(1, 1, slots_b).start()
        pieces = near.shape[0]

        def near_copy(piece, half):
            return pltpu.make_async_copy(near.at[piece], stage.at[half], stage_sem.at[half])

        near_copy(0, 0).start()
        out_ref[...] = jnp.zeros_like(out_ref)
        rows_a[...] = jnp.zeros_like(rows_a)
        rows_b[...] = jnp.zeros_like(rows_b)
        table[pl.ds(0, 2 * PAD), :] = jnp.zeros((2 * PAD, 128), jnp.float32)

        def piece_step(piece, carry):
            half = lax.rem(piece, 2)

            @pl.when(piece + 1 < pieces)
            def _():
                near_copy(piece + 1, 1 - half).start()

            near_copy(piece, half).wait()
            fill(stage.at[half], PAD + piece * chunk, chunk)
            return carry

        lax.fori_loop(0, pieces, piece_step, 0)
        base = PAD + pieces * chunk
        for part in range(top.shape[0]):
            copy = pltpu.make_async_copy(top.at[part], stage.at[0, pl.ds(0, top_chunk)], stage_sem.at[0])
            copy.start()
            copy.wait()
            fill(stage.at[0], base + part * top_chunk, top_chunk)

    def pick(into, buffer, which):
        for r in range(count):
            into[pl.ds(2 * r, 2), :] = table[pl.ds(buffer[which, r], 2), :]

    def apply(picked, which):
        head = picked[pl.ds(0, count, stride=2), :].astype(jnp.bfloat16)
        tail = picked[pl.ds(1, count, stride=2), :].astype(jnp.bfloat16)
        op = jnp.concatenate([w_ref[which], jnp.zeros((256 - width, width), jnp.bfloat16)], axis=0)
        both = jnp.concatenate([head, tail], axis=1)
        out_ref[...] += jnp.dot(both, op, preferred_element_type=jnp.float32)

    slot_copy(0, 0, slots_a).wait()
    pick(rows_a, slots_a, 0)
    apply(rows_a, 0)
    pick(rows_b, slots_a, 1)
    apply(rows_b, 1)
    slot_copy(jnp.minimum(2 * step + 2, 2 * steps - 2), 0, slots_a).start()
    slot_copy(0, 1, slots_b).wait()
    pick(rows_a, slots_b, 0)
    apply(rows_a, 2)
    pick(rows_b, slots_b, 1)
    apply(rows_b, 3)
    slot_copy(jnp.minimum(2 * step + 3, 2 * steps - 1), 1, slots_b).start()

    @pl.when(step == steps - 1)
    def _():
        slot_copy(0, 0, slots_a).wait()
        slot_copy(0, 1, slots_b).wait()


def far_field(slots, near, top, m2l_ops):
    vectors, count = slots.shape
    pieces, chunk, width = near.shape
    table_rows = PAD + pieces * chunk + top.shape[0] * top.shape[1]
    return pl.pallas_call(
        far_kernel,
        grid=(vectors // 4,),
        in_specs=[
            pl.BlockSpec(memory_space=pl.ANY),
            pl.BlockSpec(memory_space=pl.ANY),
            pl.BlockSpec(memory_space=pl.ANY),
            pl.BlockSpec((4, width, width), lambda s: (s, 0, 0)),
        ],
        out_specs=pl.BlockSpec((count, width), lambda s: (0, 0)),
        out_shape=jax.ShapeDtypeStruct((count, width), jnp.float32),
        scratch_shapes=[
            pltpu.VMEM((2 * table_rows, 128), jnp.float32),
            pltpu.VMEM((2 * count, 128), jnp.float32),
            pltpu.VMEM((2 * count, 128), jnp.float32),
            pltpu.VMEM((2, chunk, width), jnp.bfloat16),
            pltpu.SMEM((2, count), jnp.int32),
            pltpu.SMEM((2, count), jnp.int32),
            pltpu.SemaphoreType.DMA((2,)),
            pltpu.SemaphoreType.DMA((2,)),
        ],
        compiler_params=pltpu.CompilerParams(vmem_limit_bytes=56 * 2**20),
        name="far_field",
    )(slots.reshape(vectors // 2, 2, count), near, top, m2l_ops)


def local(leaf_mult, leaf_list, parent_list, top_list, m2m_ops, m2l_ops, l2l_ops):
    boxes, width = leaf_mult.shape
    vectors = leaf_list.shape[1]
    here = lax.axis_index("morton")
    devices = lax.axis_size("morton")
    parents, tops = boxes // 8, boxes // 64
    chunk = boxes + parents
    parent_mult = ascend(leaf_mult, m2m_ops)
    piece = jnp.concatenate([leaf_mult, parent_mult], axis=0)
    three = jnp.stack([shifted(piece, "morton", RD), piece, shifted(piece, "morton", -RD)])
    groups = [list(range(g, g + RD)) for g in range(0, devices, RD)]
    near = lax.all_gather(three, "morton", axis=0, tiled=True, axis_index_groups=groups)
    top_mult = ascend(parent_mult, m2m_ops)
    all_top = lax.all_gather(top_mult, "morton", axis=0, tiled=True)

    def place(box, per_device):
        device = box // per_device
        return ((device % RD) * 3 + device // RD - here // RD + 1) * chunk + box % per_device

    leaf_row = here * boxes + jnp.arange(boxes, dtype=jnp.int32)[None, :]
    leaf_offset = leaf_list.T
    leaf_slot = jnp.where(leaf_offset != 0, PAD + place(leaf_row + leaf_offset, boxes), 0)
    parent_box = parent_list.T
    parent_slot = jnp.where(parent_box >= 0, PAD + boxes + place(parent_box, parents), 0)
    top_box = top_list.T
    top_slot = jnp.where(top_box >= 0, PAD + 3 * RD * chunk + top_box, 0)
    spare = -(boxes + parents + tops) % 16
    slots = 2 * jnp.concatenate([leaf_slot, parent_slot, top_slot, jnp.zeros((vectors, spare), jnp.int32)], axis=1)
    far = far_field(slots, near, all_top.reshape(2, -1, width), m2l_ops)
    leaf_far = far[:boxes]
    parent_far = far[boxes:chunk]
    top_far = far[chunk : chunk + tops]
    top_local = (0.25 * top_far).astype(jnp.bfloat16)
    parent_local = (0.5 * parent_far + descend(top_local, l2l_ops)).astype(jnp.bfloat16)
    return leaf_far + descend(parent_local, l2l_ops)


def solution(mesh):
    return jax.shard_map(
        local,
        mesh=mesh,
        in_specs=(
            P("morton", None),
            P("morton", None),
            P("morton", None),
            P("morton", None),
            P(),
            P(),
            P(),
        ),
        out_specs=P("morton", None),
        check_vma=False,
    )
```

```python
import jax
import jax.numpy as jnp
from jax import lax
from jax.experimental import pallas as pl
from jax.experimental.pallas import tpu as pltpu
from jax.sharding import PartitionSpec as P

RD = 8
PAD = 8
GROUP = 4
TOP_ROWS = 16


def shifted(block, axis, distance):
    devices = range(lax.axis_size(axis))
    route = [(i - distance, i) for i in devices if i - distance in devices]
    return lax.ppermute(block, axis, route)


def ascend(children, m2m_ops):
    width = children.shape[1]
    grouped = children.reshape(children.shape[0] // 8, 8 * width)
    summed = jnp.dot(grouped, m2m_ops.reshape(8 * width, width), preferred_element_type=jnp.float32)
    return summed.astype(jnp.bfloat16)


def descend(coarse, l2l_ops):
    spread = jnp.einsum("tq,cqp->tcp", coarse, l2l_ops, preferred_element_type=jnp.float32)
    return spread.reshape(coarse.shape[0] * 8, coarse.shape[1])


def far_kernel(slots, near, top, w_before, w_now, out_ref, table, rows_a, rows_b, stage, top_stage, slots_a, slots_b, sem, stage_sem):
    step = pl.program_id(0)
    steps = pl.num_programs(0)
    groups = slots.shape[0]
    count, width = out_ref.shape

    def slot_copy(group, which, buffer):
        return pltpu.make_async_copy(slots.at[group], buffer, sem.at[which])

    def fill(buffer, base):
        rows, wide = buffer.shape

        def sixteen(j, carry):
            x = buffer[pl.ds(pl.multiple_of(16 * j, 16), 16), :].astype(jnp.float32)
            tail = x[:, 128:]
            if wide < 256:
                tail = jnp.concatenate([tail, jnp.zeros((16, 256 - wide), jnp.float32)], axis=1)
            start = 2 * (base + 16 * j)
            table[pl.ds(start, 16, stride=2), :] = x[:, :128]
            table[pl.ds(start + 1, 16, stride=2), :] = tail
            return carry

        lax.fori_loop(0, rows // 16, sixteen, 0, unroll=2)

    def fill_all(pieces, source, buffers, base):
        def copy(piece, half):
            return pltpu.make_async_copy(source.at[piece], buffers.at[half], stage_sem.at[half])

        copy(0, 0).start()

        def one(piece, carry):
            half = lax.rem(piece, 2)

            @pl.when(piece + 1 < pieces)
            def _():
                copy(piece + 1, 1 - half).start()

            copy(piece, half).wait()
            fill(buffers.at[half], base + piece * buffers.shape[1])
            return carry

        lax.fori_loop(0, pieces, one, 0)

    @pl.when(step == 0)
    def _():
        slot_copy(0, 0, slots_a).start()
        slot_copy(1, 1, slots_b).start()
        out_ref[...] = jnp.zeros_like(out_ref)
        rows_b[...] = jnp.zeros_like(rows_b)
        table[pl.ds(0, 2 * PAD), :] = jnp.zeros((2 * PAD, 128), jnp.float32)
        fill_all(near.shape[0], near, stage, PAD)
        fill_all(top.shape[0], top, top_stage, PAD + near.shape[0] * near.shape[1])

    def pick(into, buffer):
        for g in range(GROUP):
            for r in range(count):
                into[g, pl.ds(2 * r, 2), :] = table[pl.ds(buffer[g, r], 2), :]

    def apply(picked, w_ref):
        parts, ops = [], []
        for g in range(GROUP):
            parts.append(picked[g, pl.ds(0, count, stride=2), :].astype(jnp.bfloat16))
            parts.append(picked[g, pl.ds(1, count, stride=2), :].astype(jnp.bfloat16))
            ops.append(w_ref[g])
            ops.append(jnp.zeros((256 - width, width), jnp.bfloat16))
        out_ref[...] += jnp.dot(
            jnp.concatenate(parts, axis=1), jnp.concatenate(ops, axis=0), preferred_element_type=jnp.float32
        )

    slot_copy(0, 0, slots_a).wait()
    pick(rows_a, slots_a)
    apply(rows_b, w_before)
    slot_copy(jnp.minimum(2 * step + 2, groups - 1), 0, slots_a).start()
    slot_copy(0, 1, slots_b).wait()
    pick(rows_b, slots_b)
    apply(rows_a, w_now)
    slot_copy(jnp.minimum(2 * step + 3, groups - 1), 1, slots_b).start()

    @pl.when(step == steps - 1)
    def _():
        slot_copy(0, 0, slots_a).wait()
        slot_copy(0, 1, slots_b).wait()


def far_field(slots, near, top, m2l_ops):
    vectors, count = slots.shape
    pieces, chunk, width = near.shape
    groups = vectors // GROUP
    table_rows = PAD + pieces * chunk + top.shape[0] * top.shape[1]
    return pl.pallas_call(
        far_kernel,
        grid=((groups + 1) // 2,),
        in_specs=[
            pl.BlockSpec(memory_space=pl.ANY),
            pl.BlockSpec(memory_space=pl.ANY),
            pl.BlockSpec(memory_space=pl.ANY),
            pl.BlockSpec((GROUP, width, width), lambda s: (jnp.maximum(2 * s - 1, 0), 0, 0)),
            pl.BlockSpec((GROUP, width, width), lambda s: (2 * s, 0, 0)),
        ],
        out_specs=pl.BlockSpec((count, width), lambda s: (0, 0)),
        out_shape=jax.ShapeDtypeStruct((count, width), jnp.float32),
        scratch_shapes=[
            pltpu.VMEM((2 * table_rows, 128), jnp.float32),
            pltpu.VMEM((GROUP, 2 * count, 128), jnp.float32),
            pltpu.VMEM((GROUP, 2 * count, 128), jnp.float32),
            pltpu.VMEM((2, chunk, width), jnp.bfloat16),
            pltpu.VMEM((2,) + top.shape[1:], jnp.bfloat16),
            pltpu.SMEM((GROUP, count), jnp.int32),
            pltpu.SMEM((GROUP, count), jnp.int32),
            pltpu.SemaphoreType.DMA((2,)),
            pltpu.SemaphoreType.DMA((2,)),
        ],
        compiler_params=pltpu.CompilerParams(vmem_limit_bytes=56 * 2**20),
        name="far_field",
    )(slots.reshape(groups, GROUP, count), near, top, m2l_ops, m2l_ops)


def local(leaf_mult, leaf_list, parent_list, top_list, m2m_ops, m2l_ops, l2l_ops):
    boxes, width = leaf_mult.shape
    vectors = leaf_list.shape[1]
    here = lax.axis_index("morton")
    devices = lax.axis_size("morton")
    parents, tops = boxes // 8, boxes // 64
    chunk = boxes + parents
    parent_mult = ascend(leaf_mult, m2m_ops)
    piece = jnp.concatenate([leaf_mult, parent_mult], axis=0)
    three = jnp.stack([shifted(piece, "morton", RD), piece, shifted(piece, "morton", -RD)])
    groups = [list(range(g, g + RD)) for g in range(0, devices, RD)]
    near = lax.all_gather(three, "morton", axis=0, tiled=True, axis_index_groups=groups)
    top_mult = ascend(parent_mult, m2m_ops)
    padded_top = jnp.pad(top_mult, ((0, TOP_ROWS - tops), (0, 256 - width)))[None]
    all_top = lax.all_gather(padded_top, "morton", axis=0, tiled=True)

    def place(box, per_device):
        device = box // per_device
        return ((device % RD) * 3 + device // RD - here // RD + 1) * chunk + box % per_device

    leaf_row = here * boxes + jnp.arange(boxes, dtype=jnp.int32)[None, :]
    leaf_offset = leaf_list.T
    leaf_slot = jnp.where(leaf_offset != 0, PAD + place(leaf_row + leaf_offset, boxes), 0)
    parent_box = parent_list.T
    parent_slot = jnp.where(parent_box >= 0, PAD + boxes + place(parent_box, parents), 0)
    top_box = top_list.T
    top_slot = jnp.where(top_box >= 0, PAD + 3 * RD * chunk + top_box // tops * TOP_ROWS + top_box % tops, 0)
    spare = -(boxes + parents + tops) % 16
    slots = 2 * jnp.concatenate([leaf_slot, parent_slot, top_slot, jnp.zeros((vectors, spare), jnp.int32)], axis=1)
    far = far_field(slots, near, all_top.reshape(2, -1, 256), m2l_ops)
    leaf_far = far[:boxes]
    parent_far = far[boxes:chunk]
    top_far = far[chunk : chunk + tops]
    top_local = (0.25 * top_far).astype(jnp.bfloat16)
    parent_local = (0.5 * parent_far + descend(top_local, l2l_ops)).astype(jnp.bfloat16)
    return leaf_far + descend(parent_local, l2l_ops)


def solution(mesh):
    return jax.shard_map(
        local,
        mesh=mesh,
        in_specs=(
            P("morton", None),
            P("morton", None),
            P("morton", None),
            P("morton", None),
            P(),
            P(),
            P(),
        ),
        out_specs=P("morton", None),
        check_vma=False,
    )
```

```python
import jax
import jax.numpy as jnp
from jax import lax
from jax.experimental import pallas as pl
from jax.experimental.pallas import tpu as pltpu
from jax.sharding import PartitionSpec as P

RD = 8
PAD = 8
GROUP = 4


def shifted(block, axis, distance):
    devices = range(lax.axis_size(axis))
    route = [(i - distance, i) for i in devices if i - distance in devices]
    return lax.ppermute(block, axis, route)


def ascend(children, m2m_ops):
    width = children.shape[1]
    grouped = children.reshape(children.shape[0] // 8, 8 * width)
    summed = jnp.dot(grouped, m2m_ops.reshape(8 * width, width), preferred_element_type=jnp.float32)
    return summed.astype(jnp.bfloat16)


def descend(coarse, l2l_ops):
    spread = jnp.einsum("tq,cqp->tcp", coarse, l2l_ops, preferred_element_type=jnp.float32)
    return spread.reshape(coarse.shape[0] * 8, coarse.shape[1])


def far_kernel(slots, near, top, w_0, w_1, w_2, out_ref, table, rows_0, rows_1, rows_2, stage, slots_0, slots_1, slots_2, sem, stage_sem):
    step = pl.program_id(0)
    steps = pl.num_programs(0)
    groups = slots.shape[0]
    count, width = out_ref.shape

    picked_rows = (rows_0, rows_1, rows_2)
    slot_buffers = (slots_0, slots_1, slots_2)
    ops_of = (w_0, w_1, w_2)

    def slot_copy(group, which):
        return pltpu.make_async_copy(slots.at[group], slot_buffers[which], sem.at[which])

    def fill(buffer, base):
        rows, wide = buffer.shape

        def sixteen(j, carry):
            x = buffer[pl.ds(pl.multiple_of(16 * j, 16), 16), :].astype(jnp.float32)
            tail = x[:, 128:]
            if wide < 256:
                tail = jnp.concatenate([tail, jnp.zeros((16, 256 - wide), jnp.float32)], axis=1)
            start = 2 * (base + 16 * j)
            table[pl.ds(start, 16, stride=2), :] = x[:, :128]
            table[pl.ds(start + 1, 16, stride=2), :] = tail
            return carry

        lax.fori_loop(0, rows // 16, sixteen, 0, unroll=6)

    def fill_all(pieces, source, buffers, base):
        def copy(piece, half):
            return pltpu.make_async_copy(source.at[piece], buffers.at[half], stage_sem.at[half])

        copy(0, 0).start()

        def one(piece, carry):
            half = lax.rem(piece, 2)

            @pl.when(piece + 1 < pieces)
            def _():
                copy(piece + 1, 1 - half).start()

            copy(piece, half).wait()
            fill(buffers.at[half], base + piece * buffers.shape[1])
            return carry

        lax.fori_loop(0, pieces, one, 0)

    @pl.when(step == 0)
    def _():
        slot_copy(0, 0).start()
        slot_copy(1, 1).start()
        out_ref[...] = jnp.zeros_like(out_ref)
        rows_2[...] = jnp.zeros_like(rows_2)
        table[pl.ds(0, 2 * PAD), :] = jnp.zeros((2 * PAD, 128), jnp.float32)
        pieces, chunk, _ = near.shape
        fill_all(pieces, near, stage, PAD)
        fill_all(top.shape[0], top, stage.at[:, pl.ds(0, top.shape[1])], PAD + pieces * chunk)

    def pick(into, buffer):
        for g in range(GROUP):
            for r in range(count):
                into[g, pl.ds(2 * r, 2), :] = table[pl.ds(buffer[g, r], 2), :]

    def apply(picked, w_ref):
        parts, ops = [], []
        for g in range(GROUP):
            parts.append(picked[g, pl.ds(0, count, stride=2), :].astype(jnp.bfloat16))
            parts.append(picked[g, pl.ds(1, count, stride=2), :].astype(jnp.bfloat16))
            ops.append(w_ref[g])
            ops.append(jnp.zeros((256 - width, width), jnp.bfloat16))
        out_ref[...] += jnp.dot(
            jnp.concatenate(parts, axis=1), jnp.concatenate(ops, axis=0), preferred_element_type=jnp.float32
        )

    for third in range(3):
        later = (third + 2) % 3
        slot_copy(0, third).wait()
        slot_copy(jnp.minimum(3 * step + third + 2, groups - 1), later).start()
        pick(picked_rows[third], slot_buffers[third])
        apply(picked_rows[later], ops_of[third])

    @pl.when(step == steps - 1)
    def _():
        slot_copy(0, 0).wait()
        slot_copy(0, 1).wait()


def far_field(slots, near, top, m2l_ops):
    vectors, count = slots.shape
    pieces, chunk, width = near.shape
    groups = vectors // GROUP
    steps = (groups + 3) // 3
    last = groups - 1
    table_rows = PAD + pieces * chunk + top.shape[0] * top.shape[1]
    grouped = jnp.pad(slots.reshape(groups, GROUP, count), ((0, 3 * steps - groups), (0, 0), (0, 0)))
    block = (GROUP, width, width)
    return pl.pallas_call(
        far_kernel,
        grid=(steps,),
        in_specs=[
            pl.BlockSpec(memory_space=pl.ANY),
            pl.BlockSpec(memory_space=pl.ANY),
            pl.BlockSpec(memory_space=pl.ANY),
            pl.BlockSpec(block, lambda s: (jnp.maximum(3 * s - 1, 0), 0, 0)),
            pl.BlockSpec(block, lambda s: (jnp.minimum(3 * s, last), 0, 0)),
            pl.BlockSpec(block, lambda s: (jnp.minimum(3 * s + 1, last), 0, 0)),
        ],
        out_specs=pl.BlockSpec((count, width), lambda s: (0, 0)),
        out_shape=jax.ShapeDtypeStruct((count, width), jnp.float32),
        scratch_shapes=[
            pltpu.VMEM((2 * table_rows, 128), jnp.float32),
            pltpu.VMEM((GROUP, 2 * count, 128), jnp.float32),
            pltpu.VMEM((GROUP, 2 * count, 128), jnp.float32),
            pltpu.VMEM((GROUP, 2 * count, 128), jnp.float32),
            pltpu.VMEM((2, chunk, width), jnp.bfloat16),
            pltpu.SMEM((GROUP, count), jnp.int32),
            pltpu.SMEM((GROUP, count), jnp.int32),
            pltpu.SMEM((GROUP, count), jnp.int32),
            pltpu.SemaphoreType.DMA((3,)),
            pltpu.SemaphoreType.DMA((2,)),
        ],
        compiler_params=pltpu.CompilerParams(vmem_limit_bytes=56 * 2**20),
        name="far_field",
    )(grouped, near, top, m2l_ops, m2l_ops, m2l_ops)


def local(leaf_mult, leaf_list, parent_list, top_list, m2m_ops, m2l_ops, l2l_ops):
    boxes, width = leaf_mult.shape
    vectors = leaf_list.shape[1]
    here = lax.axis_index("morton")
    devices = lax.axis_size("morton")
    parents, tops = boxes // 8, boxes // 64
    chunk = boxes + parents
    parent_mult = ascend(leaf_mult, m2m_ops)
    piece = jnp.concatenate([leaf_mult, parent_mult], axis=0)
    three = jnp.stack([shifted(piece, "morton", RD), piece, shifted(piece, "morton", -RD)])
    groups = [list(range(g, g + RD)) for g in range(0, devices, RD)]
    near = lax.all_gather(three, "morton", axis=0, tiled=True, axis_index_groups=groups)
    top_mult = ascend(parent_mult, m2m_ops)
    group_top = lax.all_gather(top_mult, "morton", axis=0, tiled=True, axis_index_groups=groups)
    strides = [list(range(g, devices, RD)) for g in range(RD)]
    all_top = lax.all_gather(group_top, "morton", axis=0, tiled=True, axis_index_groups=strides)

    def place(box, per_device):
        device = box // per_device
        return ((device % RD) * 3 + device // RD - here // RD + 1) * chunk + box % per_device

    leaf_row = here * boxes + jnp.arange(boxes, dtype=jnp.int32)[None, :]
    leaf_offset = leaf_list.T
    leaf_slot = jnp.where(leaf_offset != 0, PAD + place(leaf_row + leaf_offset, boxes), 0)
    parent_box = parent_list.T
    parent_slot = jnp.where(parent_box >= 0, PAD + boxes + place(parent_box, parents), 0)
    top_box = top_list.T
    top_slot = jnp.where(top_box >= 0, PAD + 3 * RD * chunk + top_box, 0)
    spare = -(boxes + parents + tops) % 16
    slots = 2 * jnp.concatenate([leaf_slot, parent_slot, top_slot, jnp.zeros((vectors, spare), jnp.int32)], axis=1)
    far = far_field(slots, near, all_top.reshape(2, -1, width), m2l_ops)
    leaf_far = far[:boxes]
    parent_far = far[boxes:chunk]
    top_far = far[chunk : chunk + tops]
    top_local = (0.25 * top_far).astype(jnp.bfloat16)
    parent_local = (0.5 * parent_far + descend(top_local, l2l_ops)).astype(jnp.bfloat16)
    return leaf_far + descend(parent_local, l2l_ops)


def solution(mesh):
    return jax.shard_map(
        local,
        mesh=mesh,
        in_specs=(
            P("morton", None),
            P("morton", None),
            P("morton", None),
            P("morton", None),
            P(),
            P(),
            P(),
        ),
        out_specs=P("morton", None),
        check_vma=False,
    )
```

```python
import jax
import jax.numpy as jnp
from jax import lax
from jax.experimental import pallas as pl
from jax.experimental.pallas import tpu as pltpu
from jax.sharding import PartitionSpec as P

RD = 8
PAD = 8
GROUP = 4


def shifted(block, axis, distance):
    devices = range(lax.axis_size(axis))
    route = [(i - distance, i) for i in devices if i - distance in devices]
    return lax.ppermute(block, axis, route)


def ascend(children, m2m_ops):
    width = children.shape[1]
    grouped = children.reshape(children.shape[0] // 8, 8 * width)
    summed = jnp.dot(grouped, m2m_ops.reshape(8 * width, width), preferred_element_type=jnp.float32)
    return summed.astype(jnp.bfloat16)


def descend(coarse, l2l_ops):
    spread = jnp.einsum("tq,cqp->tcp", coarse, l2l_ops, preferred_element_type=jnp.float32)
    return spread.reshape(coarse.shape[0] * 8, coarse.shape[1])


def far_kernel(slots, near, top, w_0, w_1, w_2, out_ref, table, rows_0, rows_1, rows_2, stage, slots_0, slots_1, slots_2, sem, stage_sem):
    step = pl.program_id(0)
    steps = pl.num_programs(0)
    groups = slots.shape[0]
    count, width = out_ref.shape

    picked_rows = (rows_0, rows_1, rows_2)
    slot_buffers = (slots_0, slots_1, slots_2)
    ops_of = (w_0, w_1, w_2)

    def slot_copy(group, which):
        return pltpu.make_async_copy(slots.at[group], slot_buffers[which], sem.at[which])

    def fill(buffer, base):
        rows, wide = buffer.shape

        def sixteen(j, carry):
            x = buffer[pl.ds(pl.multiple_of(16 * j, 16), 16), :].astype(jnp.float32)
            tail = x[:, 128:]
            if wide < 256:
                tail = jnp.concatenate([tail, jnp.zeros((16, 256 - wide), jnp.float32)], axis=1)
            start = 2 * (base + 16 * j)
            table[pl.ds(start, 16, stride=2), :] = x[:, :128]
            table[pl.ds(start + 1, 16, stride=2), :] = tail
            return carry

        lax.fori_loop(0, rows // 16, sixteen, 0, unroll=6)

    def fill_all(pieces, source, buffers, base):
        def copy(piece, half):
            return pltpu.make_async_copy(source.at[piece], buffers.at[half], stage_sem.at[half])

        copy(0, 0).start()

        def one(piece, carry):
            half = lax.rem(piece, 2)

            @pl.when(piece + 1 < pieces)
            def _():
                copy(piece + 1, 1 - half).start()

            copy(piece, half).wait()
            fill(buffers.at[half], base + piece * buffers.shape[1])
            return carry

        lax.fori_loop(0, pieces, one, 0)

    @pl.when(step == 0)
    def _():
        slot_copy(0, 0).start()
        slot_copy(1, 1).start()
        out_ref[...] = jnp.zeros_like(out_ref)
        rows_2[...] = jnp.zeros_like(rows_2)
        table[pl.ds(0, 2 * PAD), :] = jnp.zeros((2 * PAD, 128), jnp.float32)
        pieces, chunk, _ = near.shape
        fill_all(pieces, near, stage, PAD)
        fill_all(top.shape[0], top, stage.at[:, pl.ds(0, top.shape[1])], PAD + pieces * chunk)

    def pick(into, buffer):
        for g in range(GROUP):
            for r in range(count):
                into[g, pl.ds(2 * r, 2), :] = table[pl.ds(buffer[g, r], 2), :]

    def apply(picked, w_ref):
        parts, ops = [], []
        for g in range(GROUP):
            parts.append(picked[g, pl.ds(0, count, stride=2), :].astype(jnp.bfloat16))
            parts.append(picked[g, pl.ds(1, count, stride=2), :].astype(jnp.bfloat16))
            ops.append(w_ref[g])
            ops.append(jnp.zeros((256 - width, width), jnp.bfloat16))
        out_ref[...] += jnp.dot(
            jnp.concatenate(parts, axis=1), jnp.concatenate(ops, axis=0), preferred_element_type=jnp.float32
        )

    for third in range(3):
        later = (third + 2) % 3
        slot_copy(0, third).wait()
        slot_copy(jnp.minimum(3 * step + third + 2, groups - 1), later).start()
        pick(picked_rows[third], slot_buffers[third])
        apply(picked_rows[later], ops_of[third])

    @pl.when(step == steps - 1)
    def _():
        slot_copy(0, 0).wait()
        slot_copy(0, 1).wait()


def far_field(slots, near, top, m2l_ops):
    vectors, count = slots.shape
    pieces, chunk, width = near.shape
    groups = vectors // GROUP
    steps = (groups + 3) // 3
    last = groups - 1
    table_rows = PAD + pieces * chunk + top.shape[0] * top.shape[1]
    grouped = jnp.pad(slots.reshape(groups, GROUP, count), ((0, 3 * steps - groups), (0, 0), (0, 0)))
    block = (GROUP, width, width)
    return pl.pallas_call(
        far_kernel,
        grid=(steps,),
        in_specs=[
            pl.BlockSpec(memory_space=pl.ANY),
            pl.BlockSpec(memory_space=pl.ANY),
            pl.BlockSpec(memory_space=pl.ANY),
            pl.BlockSpec(block, lambda s: (jnp.maximum(3 * s - 1, 0), 0, 0)),
            pl.BlockSpec(block, lambda s: (jnp.minimum(3 * s, last), 0, 0)),
            pl.BlockSpec(block, lambda s: (jnp.minimum(3 * s + 1, last), 0, 0)),
        ],
        out_specs=pl.BlockSpec((count, width), lambda s: (0, 0)),
        out_shape=jax.ShapeDtypeStruct((count, width), jnp.float32),
        scratch_shapes=[
            pltpu.VMEM((2 * table_rows, 128), jnp.float32),
            pltpu.VMEM((GROUP, 2 * count, 128), jnp.float32),
            pltpu.VMEM((GROUP, 2 * count, 128), jnp.float32),
            pltpu.VMEM((GROUP, 2 * count, 128), jnp.float32),
            pltpu.VMEM((2, chunk, width), jnp.bfloat16),
            pltpu.SMEM((GROUP, count), jnp.int32),
            pltpu.SMEM((GROUP, count), jnp.int32),
            pltpu.SMEM((GROUP, count), jnp.int32),
            pltpu.SemaphoreType.DMA((3,)),
            pltpu.SemaphoreType.DMA((2,)),
        ],
        compiler_params=pltpu.CompilerParams(vmem_limit_bytes=56 * 2**20),
        name="far_field",
    )(grouped, near, top, m2l_ops, m2l_ops, m2l_ops)


def local(leaf_mult, leaf_list, parent_list, top_list, m2m_ops, m2l_ops, l2l_ops):
    boxes, width = leaf_mult.shape
    vectors = leaf_list.shape[1]
    here = lax.axis_index("morton")
    devices = lax.axis_size("morton")
    parents, tops = boxes // 8, boxes // 64
    chunk = boxes + parents
    parent_mult = ascend(leaf_mult, m2m_ops)
    piece = jnp.concatenate([leaf_mult, parent_mult], axis=0)
    three = jnp.stack([shifted(piece, "morton", RD), piece, shifted(piece, "morton", -RD)])
    groups = [list(range(g, g + RD)) for g in range(0, devices, RD)]
    near = lax.all_gather(three, "morton", axis=0, tiled=True, axis_index_groups=groups)
    near, top_mult = lax.optimization_barrier((near, ascend(parent_mult, m2m_ops)))
    group_top = lax.all_gather(top_mult, "morton", axis=0, tiled=True, axis_index_groups=groups)
    strides = [list(range(g, devices, RD)) for g in range(RD)]
    all_top = lax.all_gather(group_top, "morton", axis=0, tiled=True, axis_index_groups=strides)

    def place(box, per_device):
        device = box // per_device
        return ((device % RD) * 3 + device // RD - here // RD + 1) * chunk + box % per_device

    leaf_row = here * boxes + jnp.arange(boxes, dtype=jnp.int32)[None, :]
    leaf_offset = leaf_list.T
    leaf_slot = jnp.where(leaf_offset != 0, PAD + place(leaf_row + leaf_offset, boxes), 0)
    parent_box = parent_list.T
    parent_slot = jnp.where(parent_box >= 0, PAD + boxes + place(parent_box, parents), 0)
    top_box = top_list.T
    top_slot = jnp.where(top_box >= 0, PAD + 3 * RD * chunk + top_box, 0)
    spare = -(boxes + parents + tops) % 16
    slots = 2 * jnp.concatenate([leaf_slot, parent_slot, top_slot, jnp.zeros((vectors, spare), jnp.int32)], axis=1)
    far = far_field(slots, near, all_top.reshape(2, -1, width), m2l_ops)
    leaf_far = far[:boxes]
    parent_far = far[boxes:chunk]
    top_far = far[chunk : chunk + tops]
    top_local = (0.25 * top_far).astype(jnp.bfloat16)
    parent_local = (0.5 * parent_far + descend(top_local, l2l_ops)).astype(jnp.bfloat16)
    return leaf_far + descend(parent_local, l2l_ops)


def solution(mesh):
    return jax.shard_map(
        local,
        mesh=mesh,
        in_specs=(
            P("morton", None),
            P("morton", None),
            P("morton", None),
            P("morton", None),
            P(),
            P(),
            P(),
        ),
        out_specs=P("morton", None),
        check_vma=False,
    )
```
